32 devices in a mesh: group: 2 (over y), freq: 4 (over z), support: 2 (over x), row: 2 (over core).
Axes of the slice: x: 2, y: 2, z: 4, core: 2. Of those that a mesh axis runs over, the one named last changes fastest.
Arguments:
- coherency: bfloat16 [4, 2048, 2048], P('freq', ('support', 'row')), as said below
- phases: int32 [4, 2048, 64], P('freq', ('support', 'row'), 'group'), parts along dimension 2, may hold values from 0 to 63
- influence: bfloat16 [2048, 2048], P(('support', 'row')), may hold values from -0.1875 to 0.1875
- mode_freq: float32 [2048], replicated, may hold values from 1 to 3
- damping: float32 [2048], replicated, may hold values from 0.3 to 0.7
- shapes: bfloat16 [2048, 2048], P(None, ('support', 'row')), may hold values from -0.1875 to 0.1875
Outputs:
- displacement: float32 [8, 64, 2048], P(None, ('group', 'freq'), ('support', 'row')), parts along dimension 1
The draws below stay inside these ranges and needn't reach their ends.
There are 2 independent parts, one for each index of `group`. The reference program is written for one: setup_inputs(seed, part) draws one part's arguments, and reference() takes and returns one part's arrays. A program takes and returns all parts, laid end to end along the dimension named above; an argument that names none is the same for every part. Nothing has to cross between parts.
Inputs may be any that keep to these rules, and one draw needn't show every extreme that they name: coherency[f] is lower triangular, with a positive diagonal between 0.8 and 1.5 that is the largest entry of each row.
All inputs are finite; a program needn't handle non-finite values.
Results may differ from the reference program's by a relative error of at most 0.018.
Values may be sent and summed in bfloat16 or wider, within the bound.
A program may use at most 64 MiB of HBM per device.

```python
import math
import jax
import jax.numpy as jnp
from jax import lax

S = 2048
M = 2048
NDOF = 2048
NPH = 64
F = 4
R = 32
N_SUPPORT = 2
N_ROW = 2


def draw_coherency(key, part):
    initial_key = jax.random.fold_in(key, 11)
    second_key = jax.random.fold_in(key, 12)
    rows_idx = jnp.arange(S)[:, None]
    cols_idx = jnp.arange(S)[None, :]
    below = (cols_idx < rows_idx).astype(jnp.float32)
    diagonal_mask = (cols_idx == rows_idx).astype(jnp.float32)
    values = jax.random.normal(initial_key, (F, S, S), jnp.float32)
    diag_gain = jax.random.uniform(second_key, (F, S, 1), jnp.float32, 0.9, 1.1)
    lower = values * below * (0.8 / jnp.sqrt(jnp.float32(S)))
    return (lower + diagonal_mask * diag_gain).astype(jnp.bfloat16)


def touch_ends(entries, rng, smallest, top_value):
    dims = entries.shape
    spot = [jax.random.randint(jax.random.fold_in(rng, axis), (), 0, dims[axis]) for axis in range(len(dims))]
    entries = entries.at[tuple(spot)].set(smallest)
    longest = dims.index(max(dims))
    spot[longest] = (spot[longest] + 1) % dims[longest]
    return entries.at[tuple(spot)].set(top_value)


def raised(result, stream_key, source, target, blocks, factor):
    owner, partner = [(jnp.arange(result.shape[dim]) // (result.shape[dim] // blocks)).reshape([-1 if axis == dim else 1 for axis in range(result.ndim)]) for dim in (source, target)]
    chosen = jax.random.permutation(stream_key, blocks)[partner]
    strong = (owner == chosen) | (owner == (partner + blocks // 2) % blocks)
    return jnp.where(strong, factor * result, result)


def block_levels(rng, dims, cuts, least, largest):
    def one(axis_at, parts):
        heights = jax.random.uniform(jax.random.fold_in(jax.random.fold_in(rng, 6), axis_at), (parts,), jnp.float32, least / len(cuts), largest / len(cuts))
        return jnp.repeat(jnp.exp(heights), dims[axis_at] // parts).reshape((-1,) + (1,) * (len(dims) - axis_at - 1))

    factor_of = one(*cuts[0])
    for cut in cuts[1:]:
        factor_of = factor_of * one(*cut)
    return factor_of


def heavy_noise(stream_key, extent, deviation, limit, split, heavy, kind=jnp.bfloat16):
    result = deviation * jax.random.normal(stream_key, extent, jnp.float32)
    if split:
        result = result * block_levels(stream_key, extent, split, -0.22, 0.18)
    return jnp.clip(raised(result, jax.random.fold_in(stream_key, 3), *heavy), -limit, limit).astype(kind)


def setup_inputs(seed: int = 0, part: int = 0) -> dict:
    splits = jax.random.split(jax.random.key(seed), 7)
    part_keys = jax.random.split(jax.random.fold_in(splits[6], part), 7)
    return {
        "coherency": draw_coherency(jax.random.fold_in(splits[6], 71), part),
        "phases": touch_ends(jax.random.randint(part_keys[1], (F, S, R), 0, NPH), jax.random.fold_in(part_keys[1], 1), 0, NPH - 1).astype(jnp.int32),
        "influence": heavy_noise(splits[2], (S, M), S ** -0.5, 0.1875, ((0, 4),), (0, 1, 4, 2.0)),
        "mode_freq": jnp.clip(jnp.exp(jax.random.uniform(splits[3], (M,), jnp.float32, math.log(1.0), math.log(3.0))), 1.0, 3.0),
        "damping": jnp.clip(jax.random.uniform(splits[4], (M,), jnp.float32, 0.3, 0.7), 0.3, 0.7),
        "shapes": heavy_noise(splits[5], (NDOF, M), M ** -0.5, 0.1875, ((1, 4),), (1, 0, 4, 2.0)),
    }


def reference(coherency, phases, influence, mode_freq, damping, shapes):
    blocks = N_SUPPORT * N_ROW
    angle = phases.astype(jnp.float32) * (2.0 * math.pi / NPH)
    table = jnp.concatenate([jnp.cos(angle), jnp.sin(angle)], -1).astype(jnp.bfloat16)
    infl_blocks = influence.reshape(blocks, S // blocks, M).astype(jnp.float32)

    def forces_one(operands):
        factor, phase_rows = operands
        power_spectra = jnp.dot(factor, phase_rows, preferred_element_type=jnp.float32).astype(jnp.bfloat16)
        power_spectra = power_spectra.reshape(blocks, S // blocks, 2 * R).astype(jnp.float32)
        partial_terms = jnp.einsum('bsm,bsr->bmr', infl_blocks, power_spectra).astype(jnp.bfloat16)
        return lax.optimization_barrier(jnp.sum(partial_terms.astype(jnp.float32), 0))
    forces = lax.map(forces_one, (coherency, table))
    omega = ((jnp.arange(F) + 1).astype(jnp.float32) * (2.5 / F))[:, None]
    mode_sq = (mode_freq * mode_freq)[None, :]
    real_den = mode_sq - omega * omega
    imag_den = 2.0 * damping[None, :] * mode_freq[None, :] * omega
    denom = real_den * real_den + imag_den * imag_den
    recep_re = (mode_sq * real_den / denom)[:, :, None]
    recep_im = (-mode_sq * imag_den / denom)[:, :, None]
    force_re = forces[:, :, :R]
    force_imaginary = forces[:, :, R:]
    resp_re = recep_re * force_re - recep_im * force_imaginary
    resp_im = recep_re * force_imaginary + recep_im * force_re
    ntime = 2 * F
    steps_n = jnp.arange(ntime).astype(jnp.int32)
    bins = (jnp.arange(F) + 1).astype(jnp.int32)
    wrapped = steps_n[:, None] * bins[None, :] % ntime
    theta = wrapped.astype(jnp.float32) * (2.0 * math.pi / ntime)
    factor_scale = jnp.float32(math.sqrt(2.0 / F))
    cos_table = jnp.cos(theta) * factor_scale
    sine_lookup_table = -jnp.sin(theta) * factor_scale
    modal = jnp.einsum('nf,fmr->nrm', cos_table, resp_re, precision=lax.Precision.HIGHEST)
    modal = modal + jnp.einsum('nf,fmr->nrm', sine_lookup_table, resp_im, precision=lax.Precision.HIGHEST)
    modal = modal.astype(jnp.bfloat16).reshape(ntime * R, M)
    mode_block = M // blocks

    def add_block(index, total):
        offset = (index * mode_block).astype(jnp.int32)
        modal_cols = lax.dynamic_slice_in_dim(modal, offset, mode_block, 1)
        shape_cols = lax.dynamic_slice_in_dim(shapes, offset, mode_block, 1)
        partial_term = lax.dot_general(modal_cols, shape_cols, (((1,), (1,)), ((), ())), preferred_element_type=jnp.float32)
        return total + partial_term.astype(jnp.bfloat16).astype(jnp.float32)
    total = lax.fori_loop(0, blocks, add_block, jnp.zeros((ntime * R, NDOF), jnp.float32))
    return total.reshape(ntime, R, NDOF)
```

```python
import functools
import math

import jax
import jax.numpy as jnp
import numpy as np
from jax import lax
from jax.experimental import pallas as pl
from jax.experimental.pallas import tpu as pltpu
from jax.sharding import PartitionSpec as P

NPH = 64
MESH = pl.DeviceIdType.MESH
NT = (((1,), (1,)), ((), ()))
NN = (((1,), (0,)), ((), ()))


def cos_sin(phase):
    quarter = NPH // 4
    quadrant = (phase + quarter // 2) // quarter
    x = (phase - quadrant * quarter).astype(jnp.float32) * (2.0 * math.pi / NPH)
    quadrant = quadrant % 4
    y = x * x
    c = 1.0 + y * (-0.5 + y * (1 / 24 + y * (-1 / 720 + y * (1 / 40320 - y * (1 / 3628800)))))
    s = x * (1.0 + y * (-1 / 6 + y * (1 / 120 + y * (-1 / 5040 + y * (1 / 362880)))))
    odd = (quadrant == 1) | (quadrant == 3)
    cos = jnp.where(odd, s, c)
    sin = jnp.where(odd, c, s)
    cos = jnp.where((quadrant == 1) | (quadrant == 2), -cos, cos)
    sin = jnp.where(quadrant >= 2, -sin, sin)
    return cos, sin


def time_factors(freq_total):
    time_total = 2 * freq_total
    wrapped = np.arange(time_total)[:, None] * (np.arange(freq_total) + 1)[None, :] % time_total
    theta = wrapped * (2.0 * math.pi / time_total)
    scale = math.sqrt(2.0 / freq_total)
    return np.cos(theta) * scale, -np.sin(theta) * scale


def kernel(
    n_support, n_row, n_freq,
    coh_in, ph_in, infl_in, mf_in, dp_in, shp_in,
    out_ref,
    coh, ph, infl, mf, dp, shp,
    tab, f_send, f_recv, r_send, r_recv, d_send, d_recv,
    local_sem, a_out, a_in, b_out, b_in, c_out, c_in, d_out, d_in,
):
    blocks = n_support * n_row
    real = ph.shape[0]
    depth = ph.shape[1]
    modes = shp.shape[1]
    real_local = real // n_freq
    dofs = shp.shape[0] // blocks
    my_support, my_row = lax.axis_index("support"), lax.axis_index("row")
    my_freq = lax.axis_index("freq")
    mine = my_support * n_row + my_row

    locals_ = [
        pltpu.make_async_copy(src, dst, local_sem.at[i])
        for i, (src, dst) in enumerate(
            [(ph_in, ph), (mf_in, mf), (dp_in, dp), (coh_in.at[0], coh), (infl_in, infl), (shp_in, shp)]
        )
    ]
    for copy in locals_:
        copy.start()

    def to_block(k):
        return {
            "support": lax.rem(my_support + k // n_row, n_support),
            "row": lax.rem(my_row + k % n_row, n_row),
        }

    def block_to(k):
        at = to_block(k)
        return at["support"] * n_row + at["row"]

    def block_from(k):
        s = lax.rem(my_support + n_support - k // n_row, n_support)
        r = lax.rem(my_row + n_row - k % n_row, n_row)
        return s * n_row + r

    def to_freq(k):
        return {"freq": lax.rem(my_freq + k, n_freq)}

    barrier = pltpu.get_barrier_semaphore()
    for k in range(1, blocks):
        pl.semaphore_signal(barrier, inc=1, device_id=to_block(k), device_id_type=MESH)
    for k in range(1, n_freq):
        pl.semaphore_signal(barrier, inc=1, device_id=to_freq(k), device_id_type=MESH)

    far_first = [k for k in range(1, blocks) if k >= n_row] + [k for k in range(1, blocks) if k < n_row]
    near_first = [k for k in range(1, blocks)]

    locals_[0].wait()
    cos, sin = cos_sin(ph[...])
    tab[0] = jnp.concatenate([cos, sin], 0).astype(jnp.bfloat16)

    pl.semaphore_wait(barrier, blocks - 1 + n_freq - 1)

    def send(src, dst, out_sem, in_sem, target):
        copy = pltpu.make_async_remote_copy(
            src_ref=src, dst_ref=dst, send_sem=out_sem, recv_sem=in_sem,
            device_id=target, device_id_type=MESH,
        )
        copy.start()
        return copy

    a_copies = {
        k: send(tab.at[0], tab.at[k], a_out.at[k], a_in.at[k], to_block(k)) for k in far_first
    }

    locals_[1].wait()
    locals_[2].wait()
    my_modes = pl.ds(pl.multiple_of(mine * modes, modes), modes)
    freq = mf[:, my_modes]
    omega = (my_freq + 1).astype(jnp.float32) * (2.5 / n_freq)
    mode_sq = freq * freq
    real_den = mode_sq - omega * omega
    imag_den = 2.0 * dp[:, my_modes] * freq * omega
    denom = real_den * real_den + imag_den * imag_den
    recep_re = mode_sq * real_den / denom
    recep_im = -mode_sq * imag_den / denom

    def spectra_term(k):
        columns = pl.ds(pl.multiple_of(block_from(k) * depth, depth), depth)
        return lax.dot_general(tab[k], coh[:, columns], NT, preferred_element_type=jnp.float32)

    locals_[3].wait()
    spectra = spectra_term(0)
    for k in near_first:
        a_copies[k].wait_recv()
        spectra += spectra_term(k)
    spectra = spectra.astype(jnp.bfloat16)

    def force_term(k):
        columns = pl.ds(pl.multiple_of(block_to(k) * modes, modes), modes)
        return lax.dot_general(
            spectra, infl[:, columns], NN, preferred_element_type=jnp.float32
        ).astype(jnp.bfloat16)

    locals_[4].wait()
    b_copies = {}
    for k in far_first:
        f_send[k] = force_term(k)
        b_copies[k] = send(f_send.at[k], f_recv.at[k], b_out.at[k], b_in.at[k], to_block(k))
    forces = force_term(0).astype(jnp.float32)
    for k in near_first:
        b_copies[k].wait_recv()
        forces += f_recv[k].astype(jnp.float32)

    force_re, force_im = forces[:real], forces[real:]
    resp_re = recep_re * force_re - recep_im * force_im
    resp_im = recep_re * force_im + recep_im * force_re
    for f in range(n_freq):
        rows = slice(f * real_local, (f + 1) * real_local)
        r_send[f] = jnp.concatenate([resp_re[rows], resp_im[rows]], 0).astype(jnp.bfloat16)
    c_copies = {
        k: send(
            r_send.at[lax.rem(my_freq + k, n_freq)], r_recv.at[my_freq],
            c_out.at[k], c_in.at[k], to_freq(k),
        )
        for k in range(1, n_freq)
    }
    r_recv[my_freq] = r_send[my_freq]
    for k in range(1, n_freq):
        c_copies[k].wait_recv()

    cos_table, sin_table = time_factors(n_freq)
    parts = [r_recv[f].astype(jnp.float32) for f in range(n_freq)]
    rows = []
    for n in range(2 * n_freq):
        total = None
        for f in range(n_freq):
            term = parts[f][:real_local] * float(cos_table[n, f])
            term += parts[f][real_local:] * float(sin_table[n, f])
            total = term if total is None else total + term
        rows.append(total)
    modal = jnp.concatenate(rows, 0).astype(jnp.bfloat16)

    def slab_term(k):
        block_rows = pl.ds(pl.multiple_of(block_to(k) * dofs, dofs), dofs)
        return lax.dot_general(
            modal, shp[block_rows, :], NT, preferred_element_type=jnp.float32
        ).astype(jnp.bfloat16)

    locals_[5].wait()
    d_copies = {}
    for k in far_first:
        d_send[k] = slab_term(k)
        d_copies[k] = send(d_send.at[k], d_recv.at[k], d_out.at[k], d_in.at[k], to_block(k))
    slab = slab_term(0).astype(jnp.float32)
    for k in near_first:
        d_copies[k].wait_recv()
        slab += d_recv[k].astype(jnp.float32)
    out_ref[...] = slab

    for copies in (a_copies, b_copies, c_copies, d_copies):
        for copy in copies.values():
            copy.wait_send()


def body(coherency, phases, influence, mode_freq, damping, shapes):
    n_support, n_row = lax.axis_size("support"), lax.axis_size("row")
    n_freq = lax.axis_size("freq")
    blocks = n_support * n_row
    depth, real = phases.shape[1], phases.shape[2]
    mode_total, modes = influence.shape[1], shapes.shape[1]
    dofs = shapes.shape[0] // blocks
    real_local = real // n_freq
    times = 2 * n_freq
    bf16, f32 = jnp.bfloat16, jnp.float32
    dma = pltpu.SemaphoreType.DMA
    slab = pl.pallas_call(
        functools.partial(kernel, n_support, n_row, n_freq),
        out_shape=jax.ShapeDtypeStruct((times * real_local, dofs), f32),
        in_specs=[pl.BlockSpec(memory_space=pltpu.HBM)] * 6,
        out_specs=pl.BlockSpec(memory_space=pltpu.VMEM),
        scratch_shapes=[
            pltpu.VMEM(coherency.shape[1:], bf16),
            pltpu.VMEM((real, depth), jnp.int32),
            pltpu.VMEM(influence.shape, bf16),
            pltpu.VMEM((1, mode_total), f32),
            pltpu.VMEM((1, mode_total), f32),
            pltpu.VMEM(shapes.shape, bf16),
            pltpu.VMEM((blocks, 2 * real, depth), bf16),
            pltpu.VMEM((blocks, 2 * real, modes), bf16),
            pltpu.VMEM((blocks, 2 * real, modes), bf16),
            pltpu.VMEM((n_freq, 2 * real_local, modes), bf16),
            pltpu.VMEM((n_freq, 2 * real_local, modes), bf16),
            pltpu.VMEM((blocks, times * real_local, dofs), bf16),
            pltpu.VMEM((blocks, times * real_local, dofs), bf16),
            dma((6,)),
            dma((blocks,)), dma((blocks,)),
            dma((blocks,)), dma((blocks,)),
            dma((n_freq,)), dma((n_freq,)),
            dma((blocks,)), dma((blocks,)),
        ],
        compiler_params=pltpu.CompilerParams(
            collective_id=0, has_side_effects=True, vmem_limit_bytes=60 * 1024 * 1024
        ),
    )(
        coherency,
        jnp.transpose(phases[0]),
        influence,
        mode_freq.reshape(1, mode_total),
        damping.reshape(1, mode_total),
        shapes,
    )
    return slab.reshape(times, real_local, dofs)


def solution(mesh):
    return jax.shard_map(
        body,
        mesh=mesh,
        in_specs=(
            P("freq", ("support", "row"), None),
            P("freq", ("support", "row"), "group"),
            P(("support", "row"), None),
            P(),
            P(),
            P(None, ("support", "row")),
        ),
        out_specs=P(None, ("group", "freq"), ("support", "row")),
        check_vma=False,
    )
```

```python
import functools
import math

import jax
import jax.numpy as jnp
import numpy as np
from jax import lax
from jax.experimental import pallas as pl
from jax.experimental.pallas import tpu as pltpu
from jax.sharding import PartitionSpec as P

NPH = 64
PIECES = 2
MESH = pl.DeviceIdType.MESH
NT = (((1,), (1,)), ((), ()))
NN = (((1,), (0,)), ((), ()))


def cos_sin(phase):
    quarter = NPH // 4
    quadrant = (phase + quarter // 2) // quarter
    x = (phase - quadrant * quarter).astype(jnp.float32) * (2.0 * math.pi / NPH)
    quadrant = quadrant % 4
    y = x * x
    c = 1.0 + y * (-0.5 + y * (1 / 24 + y * (-1 / 720 + y * (1 / 40320 - y * (1 / 3628800)))))
    s = x * (1.0 + y * (-1 / 6 + y * (1 / 120 + y * (-1 / 5040 + y * (1 / 362880)))))
    odd = (quadrant == 1) | (quadrant == 3)
    cos = jnp.where(odd, s, c)
    sin = jnp.where(odd, c, s)
    cos = jnp.where((quadrant == 1) | (quadrant == 2), -cos, cos)
    sin = jnp.where(quadrant >= 2, -sin, sin)
    return cos, sin


def time_factors(freq_total):
    time_total = 2 * freq_total
    wrapped = np.arange(time_total)[:, None] * (np.arange(freq_total) + 1)[None, :] % time_total
    theta = wrapped * (2.0 * math.pi / time_total)
    scale = math.sqrt(2.0 / freq_total)
    return np.cos(theta) * scale, -np.sin(theta) * scale


def kernel(
    n_support, n_row, n_freq,
    coh_in, ph_in, infl_in, mf_in, dp_in, shp_in,
    out_ref,
    coh, ph, infl, mf, dp, shp,
    tab, f_send, f_recv, r_send, r_recv, d_send, d_recv,
    local_sem, a_out, a_in, b_out, b_in, c_out, c_in, d_out, d_in,
):
    blocks = n_support * n_row
    real = ph.shape[0]
    depth = ph.shape[1]
    modes = shp.shape[1]
    real_local = real // n_freq
    dofs = shp.shape[0] // blocks
    my_support, my_row = lax.axis_index("support"), lax.axis_index("row")
    my_freq = lax.axis_index("freq")
    mine = my_support * n_row + my_row

    locals_ = [
        pltpu.make_async_copy(src, dst, local_sem.at[i])
        for i, (src, dst) in enumerate(
            [(ph_in, ph), (mf_in, mf), (dp_in, dp), (coh_in.at[0], coh), (infl_in, infl), (shp_in, shp)]
        )
    ]
    for copy in locals_:
        copy.start()

    def to_block(k):
        return {
            "support": lax.rem(my_support + k // n_row, n_support),
            "row": lax.rem(my_row + k % n_row, n_row),
        }

    def block_to(k):
        at = to_block(k)
        return at["support"] * n_row + at["row"]

    def block_from(k):
        s = lax.rem(my_support + n_support - k // n_row, n_support)
        r = lax.rem(my_row + n_row - k % n_row, n_row)
        return s * n_row + r

    def to_freq(k):
        return {"freq": lax.rem(my_freq + k, n_freq)}

    barrier = pltpu.get_barrier_semaphore()
    for k in range(1, blocks):
        pl.semaphore_signal(barrier, inc=1, device_id=to_block(k), device_id_type=MESH)
    for k in range(1, n_freq):
        pl.semaphore_signal(barrier, inc=1, device_id=to_freq(k), device_id_type=MESH)

    far_first = [k for k in range(1, blocks) if k >= n_row] + [k for k in range(1, blocks) if k < n_row]
    near_first = [k for k in range(1, blocks)]

    locals_[0].wait()
    cos, sin = cos_sin(ph[...])
    tab[0] = jnp.concatenate([cos, sin], 0).astype(jnp.bfloat16)

    pl.semaphore_wait(barrier, blocks - 1 + n_freq - 1)

    def send(src, dst, out_sem, in_sem, target):
        copy = pltpu.make_async_remote_copy(
            src_ref=src, dst_ref=dst, send_sem=out_sem, recv_sem=in_sem,
            device_id=target, device_id_type=MESH,
        )
        copy.start()
        return copy

    far = [k for k in far_first if k >= n_row]
    near = [k for k in near_first if k < n_row]
    rows = 2 * real // PIECES
    pieces = [pl.ds(c * rows, rows) for c in range(PIECES)]

    def send_piece(src, dst, k, c, out_sem, in_sem):
        return send(
            src.at[pieces[c]], dst.at[pieces[c]], out_sem.at[k, c], in_sem.at[k, c], to_block(k)
        )

    a_copies = {}
    for c in range(PIECES):
        for k in far + near:
            a_copies[k, c] = send_piece(tab.at[0], tab.at[k], k, c, a_out, a_in)

    locals_[1].wait()
    locals_[2].wait()
    my_modes = pl.ds(pl.multiple_of(mine * modes, modes), modes)
    freq = mf[:, my_modes]
    omega = (my_freq + 1).astype(jnp.float32) * (2.5 / n_freq)
    mode_sq = freq * freq
    real_den = mode_sq - omega * omega
    imag_den = 2.0 * dp[:, my_modes] * freq * omega
    denom = real_den * real_den + imag_den * imag_den
    recep_re = mode_sq * real_den / denom
    recep_im = -mode_sq * imag_den / denom

    def spectra_term(k, part):
        columns = pl.ds(pl.multiple_of(block_from(k) * depth, depth), depth)
        return lax.dot_general(
            tab[k, part], coh[:, columns], NT, preferred_element_type=jnp.float32
        )

    locals_[3].wait()
    whole = pl.ds(0, 2 * real)
    spectra_near = spectra_term(0, whole)
    for k in near:
        for c in range(PIECES):
            a_copies[k, c].wait_recv()
        spectra_near += spectra_term(k, whole)

    def force_term(spectra, k):
        columns = pl.ds(pl.multiple_of(block_to(k) * modes, modes), modes)
        return lax.dot_general(
            spectra, infl[:, columns], NN, preferred_element_type=jnp.float32
        ).astype(jnp.bfloat16)

    b_copies = {}
    forces = []
    for c in range(PIECES):
        spectra = spectra_near[c * rows : (c + 1) * rows]
        for k in far:
            a_copies[k, c].wait_recv()
            spectra += spectra_term(k, pieces[c])
        spectra = spectra.astype(jnp.bfloat16)
        if c == 0:
            locals_[4].wait()
        for k in far_first:
            f_send[k, pieces[c]] = force_term(spectra, k)
            b_copies[k, c] = send_piece(f_send.at[k], f_recv.at[k], k, c, b_out, b_in)
        forces.append(force_term(spectra, 0).astype(jnp.float32))
    for c in range(PIECES):
        for k in near_first:
            b_copies[k, c].wait_recv()
            forces[c] += f_recv[k, pieces[c]].astype(jnp.float32)
    forces = jnp.concatenate(forces, 0)

    force_re, force_im = forces[:real], forces[real:]
    resp_re = recep_re * force_re - recep_im * force_im
    resp_im = recep_re * force_im + recep_im * force_re
    for f in range(n_freq):
        rows = slice(f * real_local, (f + 1) * real_local)
        r_send[f] = jnp.concatenate([resp_re[rows], resp_im[rows]], 0).astype(jnp.bfloat16)
    c_copies = {
        k: send(
            r_send.at[lax.rem(my_freq + k, n_freq)], r_recv.at[my_freq],
            c_out.at[k], c_in.at[k], to_freq(k),
        )
        for k in range(1, n_freq)
    }
    r_recv[my_freq] = r_send[my_freq]
    for k in range(1, n_freq):
        c_copies[k].wait_recv()

    cos_table, sin_table = time_factors(n_freq)
    parts = [r_recv[f].astype(jnp.float32) for f in range(n_freq)]
    rows = []
    for n in range(2 * n_freq):
        total = None
        for f in range(n_freq):
            term = parts[f][:real_local] * float(cos_table[n, f])
            term += parts[f][real_local:] * float(sin_table[n, f])
            total = term if total is None else total + term
        rows.append(total)
    modal = jnp.concatenate(rows, 0).astype(jnp.bfloat16)

    def slab_term(k):
        block_rows = pl.ds(pl.multiple_of(block_to(k) * dofs, dofs), dofs)
        return lax.dot_general(
            modal, shp[block_rows, :], NT, preferred_element_type=jnp.float32
        ).astype(jnp.bfloat16)

    locals_[5].wait()
    d_copies = {}
    for k in far_first:
        d_send[k] = slab_term(k)
        d_copies[k] = send(d_send.at[k], d_recv.at[k], d_out.at[k], d_in.at[k], to_block(k))
    slab = slab_term(0).astype(jnp.float32)
    for k in near_first:
        d_copies[k].wait_recv()
        slab += d_recv[k].astype(jnp.float32)
    out_ref[...] = slab

    for copies in (a_copies, b_copies, c_copies, d_copies):
        for copy in copies.values():
            copy.wait_send()


def body(coherency, phases, influence, mode_freq, damping, shapes):
    n_support, n_row = lax.axis_size("support"), lax.axis_size("row")
    n_freq = lax.axis_size("freq")
    blocks = n_support * n_row
    depth, real = phases.shape[1], phases.shape[2]
    mode_total, modes = influence.shape[1], shapes.shape[1]
    dofs = shapes.shape[0] // blocks
    real_local = real // n_freq
    times = 2 * n_freq
    bf16, f32 = jnp.bfloat16, jnp.float32
    dma = pltpu.SemaphoreType.DMA
    slab = pl.pallas_call(
        functools.partial(kernel, n_support, n_row, n_freq),
        out_shape=jax.ShapeDtypeStruct((times * real_local, dofs), f32),
        in_specs=[pl.BlockSpec(memory_space=pltpu.HBM)] * 6,
        out_specs=pl.BlockSpec(memory_space=pltpu.VMEM),
        scratch_shapes=[
            pltpu.VMEM(coherency.shape[1:], bf16),
            pltpu.VMEM((real, depth), jnp.int32),
            pltpu.VMEM(influence.shape, bf16),
            pltpu.VMEM((1, mode_total), f32),
            pltpu.VMEM((1, mode_total), f32),
            pltpu.VMEM(shapes.shape, bf16),
            pltpu.VMEM((blocks, 2 * real, depth), bf16),
            pltpu.VMEM((blocks, 2 * real, modes), bf16),
            pltpu.VMEM((blocks, 2 * real, modes), bf16),
            pltpu.VMEM((n_freq, 2 * real_local, modes), bf16),
            pltpu.VMEM((n_freq, 2 * real_local, modes), bf16),
            pltpu.VMEM((blocks, times * real_local, dofs), bf16),
            pltpu.VMEM((blocks, times * real_local, dofs), bf16),
            dma((6,)),
            dma((blocks, PIECES)), dma((blocks, PIECES)),
            dma((blocks, PIECES)), dma((blocks, PIECES)),
            dma((n_freq,)), dma((n_freq,)),
            dma((blocks,)), dma((blocks,)),
        ],
        compiler_params=pltpu.CompilerParams(
            collective_id=0, has_side_effects=True, vmem_limit_bytes=60 * 1024 * 1024
        ),
    )(
        coherency,
        jnp.transpose(phases[0]),
        influence,
        mode_freq.reshape(1, mode_total),
        damping.reshape(1, mode_total),
        shapes,
    )
    return slab.reshape(times, real_local, dofs)


def solution(mesh):
    return jax.shard_map(
        body,
        mesh=mesh,
        in_specs=(
            P("freq", ("support", "row"), None),
            P("freq", ("support", "row"), "group"),
            P(("support", "row"), None),
            P(),
            P(),
            P(None, ("support", "row")),
        ),
        out_specs=P(None, ("group", "freq"), ("support", "row")),
        check_vma=False,
    )
```

```python
import functools
import math

import jax
import jax.numpy as jnp
import numpy as np
from jax import lax
from jax.experimental import pallas as pl
from jax.experimental.pallas import tpu as pltpu
from jax.sharding import PartitionSpec as P

NPH = 64
PIECES = 2
MESH = pl.DeviceIdType.MESH
NT = (((1,), (1,)), ((), ()))
NN = (((1,), (0,)), ((), ()))


def cos_sin(phase):
    quarter = NPH // 4
    quadrant = (phase + quarter // 2) // quarter
    x = (phase - quadrant * quarter).astype(jnp.float32) * (2.0 * math.pi / NPH)
    quadrant = quadrant % 4
    y = x * x
    c = 1.0 + y * (-0.5 + y * (1 / 24 + y * (-1 / 720 + y * (1 / 40320 - y * (1 / 3628800)))))
    s = x * (1.0 + y * (-1 / 6 + y * (1 / 120 + y * (-1 / 5040 + y * (1 / 362880)))))
    odd = (quadrant == 1) | (quadrant == 3)
    cos = jnp.where(odd, s, c)
    sin = jnp.where(odd, c, s)
    cos = jnp.where((quadrant == 1) | (quadrant == 2), -cos, cos)
    sin = jnp.where(quadrant >= 2, -sin, sin)
    return cos, sin


def time_factors(freq_total):
    time_total = 2 * freq_total
    wrapped = np.arange(time_total)[:, None] * (np.arange(freq_total) + 1)[None, :] % time_total
    theta = wrapped * (2.0 * math.pi / time_total)
    scale = math.sqrt(2.0 / freq_total)
    return np.cos(theta) * scale, -np.sin(theta) * scale


def kernel(
    n_support, n_row, n_freq,
    coh_in, ph_in, infl_in, mf_in, dp_in, shp_in,
    out_ref,
    coh, ph, infl, mf, dp, shp,
    shp_t, tab, f_send, f_recv, r_send, r_recv, d_send, d_recv,
    local_sem, a_out, a_in, b_out, b_in, c_out, c_in, d_out, d_in,
):
    blocks = n_support * n_row
    real = ph.shape[0]
    depth = ph.shape[1]
    modes = shp.shape[1]
    real_local = real // n_freq
    dofs = shp.shape[0] // blocks
    my_support, my_row = lax.axis_index("support"), lax.axis_index("row")
    my_freq = lax.axis_index("freq")
    mine = my_support * n_row + my_row

    locals_ = [
        pltpu.make_async_copy(src, dst, local_sem.at[i])
        for i, (src, dst) in enumerate(
            [(ph_in, ph), (mf_in, mf), (dp_in, dp), (coh_in.at[0], coh), (infl_in, infl), (shp_in, shp)]
        )
    ]
    for copy in locals_:
        copy.start()

    def to_block(k):
        return {
            "support": lax.rem(my_support + k // n_row, n_support),
            "row": lax.rem(my_row + k % n_row, n_row),
        }

    def block_to(k):
        at = to_block(k)
        return at["support"] * n_row + at["row"]

    def block_from(k):
        s = lax.rem(my_support + n_support - k // n_row, n_support)
        r = lax.rem(my_row + n_row - k % n_row, n_row)
        return s * n_row + r

    def to_freq(k):
        return {"freq": lax.rem(my_freq + k, n_freq)}

    barrier = pltpu.get_barrier_semaphore()
    for k in range(1, blocks):
        pl.semaphore_signal(barrier, inc=1, device_id=to_block(k), device_id_type=MESH)
    for k in range(1, n_freq):
        pl.semaphore_signal(barrier, inc=1, device_id=to_freq(k), device_id_type=MESH)

    straight = [k for k in range(n_row, blocks) if k % n_row == 0]
    far_first = straight + list(range(1, n_row))
    far_first += [k for k in range(n_row, blocks) if k % n_row]
    near_first = [k for k in range(1, blocks)]

    locals_[0].wait()
    cos, sin = cos_sin(ph[...])
    tab[0] = jnp.concatenate([cos, sin], 0).astype(jnp.bfloat16)

    pl.semaphore_wait(barrier, blocks - 1 + n_freq - 1)

    def send(src, dst, out_sem, in_sem, target):
        copy = pltpu.make_async_remote_copy(
            src_ref=src, dst_ref=dst, send_sem=out_sem, recv_sem=in_sem,
            device_id=target, device_id_type=MESH,
        )
        copy.start()
        return copy

    far = [k for k in far_first if k >= n_row]
    near = [k for k in near_first if k < n_row]
    rows = 2 * real // PIECES
    pieces = [pl.ds(c * rows, rows) for c in range(PIECES)]

    def send_piece(src, dst, k, c, out_sem, in_sem):
        return send(
            src.at[pieces[c]], dst.at[pieces[c]], out_sem.at[k, c], in_sem.at[k, c], to_block(k)
        )

    a_copies = {}
    for c in range(PIECES):
        for k in far_first:
            a_copies[k, c] = send_piece(tab.at[0], tab.at[k], k, c, a_out, a_in)

    locals_[1].wait()
    locals_[2].wait()
    my_modes = pl.ds(pl.multiple_of(mine * modes, modes), modes)
    freq = mf[:, my_modes]
    omega = (my_freq + 1).astype(jnp.float32) * (2.5 / n_freq)
    mode_sq = freq * freq
    real_den = mode_sq - omega * omega
    imag_den = 2.0 * dp[:, my_modes] * freq * omega
    denom = real_den * real_den + imag_den * imag_den
    recep_re = mode_sq * real_den / denom
    recep_im = -mode_sq * imag_den / denom

    def spectra_term(k, part):
        columns = pl.ds(pl.multiple_of(block_from(k) * depth, depth), depth)
        return lax.dot_general(
            tab[k, part], coh[:, columns], NT, preferred_element_type=jnp.float32
        )

    locals_[3].wait()
    whole = pl.ds(0, 2 * real)
    spectra_near = spectra_term(0, whole)
    for k in near:
        for c in range(PIECES):
            a_copies[k, c].wait_recv()
        spectra_near += spectra_term(k, whole)

    def force_term(spectra, k):
        columns = pl.ds(pl.multiple_of(block_to(k) * modes, modes), modes)
        return lax.dot_general(
            spectra, infl[:, columns], NN, preferred_element_type=jnp.float32
        ).astype(jnp.bfloat16)

    b_copies = {}
    forces = []
    for c in range(PIECES):
        spectra = spectra_near[c * rows : (c + 1) * rows]
        for k in far:
            a_copies[k, c].wait_recv()
            spectra += spectra_term(k, pieces[c])
        spectra = spectra.astype(jnp.bfloat16)
        if c == 0:
            locals_[4].wait()
        for k in far_first:
            f_send[k, pieces[c]] = force_term(spectra, k)
            b_copies[k, c] = send_piece(f_send.at[k], f_recv.at[k], k, c, b_out, b_in)
        forces.append(force_term(spectra, 0).astype(jnp.float32))
    locals_[5].wait()
    for b in range(blocks):
        block = slice(b * dofs, (b + 1) * dofs)
        shp_t[:, block] = shp[block, :].T
    for c in range(PIECES):
        for k in near_first:
            b_copies[k, c].wait_recv()
            forces[c] += f_recv[k, pieces[c]].astype(jnp.float32)
    forces = jnp.concatenate(forces, 0)

    force_re, force_im = forces[:real], forces[real:]
    resp_re = recep_re * force_re - recep_im * force_im
    resp_im = recep_re * force_im + recep_im * force_re
    for f in range(n_freq):
        rows = slice(f * real_local, (f + 1) * real_local)
        r_send[f] = jnp.concatenate([resp_re[rows], resp_im[rows]], 0).astype(jnp.bfloat16)
    c_copies = {
        k: send(
            r_send.at[lax.rem(my_freq + k, n_freq)], r_recv.at[my_freq],
            c_out.at[k], c_in.at[k], to_freq(k),
        )
        for k in range(1, n_freq)
    }
    r_recv[my_freq] = r_send[my_freq]
    for k in range(1, n_freq):
        c_copies[k].wait_recv()

    cos_table, sin_table = time_factors(n_freq)
    parts = [r_recv[f].astype(jnp.float32) for f in range(n_freq)]
    rows = []
    for n in range(2 * n_freq):
        total = None
        for f in range(n_freq):
            term = parts[f][:real_local] * float(cos_table[n, f])
            term += parts[f][real_local:] * float(sin_table[n, f])
            total = term if total is None else total + term
        rows.append(total)
    modal = jnp.concatenate(rows, 0).astype(jnp.bfloat16)

    def slab_term(k):
        block_rows = pl.ds(pl.multiple_of(block_to(k) * dofs, dofs), dofs)
        return lax.dot_general(
            modal, shp_t[:, block_rows], NN, preferred_element_type=jnp.float32
        ).astype(jnp.bfloat16)

    d_copies = {}
    for k in far_first:
        d_send[k] = slab_term(k)
        d_copies[k] = send(d_send.at[k], d_recv.at[k], d_out.at[k], d_in.at[k], to_block(k))
    slab = slab_term(0).astype(jnp.float32)
    for k in near_first:
        d_copies[k].wait_recv()
        slab += d_recv[k].astype(jnp.float32)
    out_ref[...] = slab

    for copies in (a_copies, b_copies, c_copies, d_copies):
        for copy in copies.values():
            copy.wait_send()


def body(coherency, phases, influence, mode_freq, damping, shapes):
    n_support, n_row = lax.axis_size("support"), lax.axis_size("row")
    n_freq = lax.axis_size("freq")
    blocks = n_support * n_row
    depth, real = phases.shape[1], phases.shape[2]
    mode_total, modes = influence.shape[1], shapes.shape[1]
    dofs = shapes.shape[0] // blocks
    real_local = real // n_freq
    times = 2 * n_freq
    bf16, f32 = jnp.bfloat16, jnp.float32
    dma = pltpu.SemaphoreType.DMA
    slab = pl.pallas_call(
        functools.partial(kernel, n_support, n_row, n_freq),
        out_shape=jax.ShapeDtypeStruct((times * real_local, dofs), f32),
        in_specs=[pl.BlockSpec(memory_space=pltpu.HBM)] * 6,
        out_specs=pl.BlockSpec(memory_space=pltpu.VMEM),
        scratch_shapes=[
            pltpu.VMEM(coherency.shape[1:], bf16),
            pltpu.VMEM((real, depth), jnp.int32),
            pltpu.VMEM(influence.shape, bf16),
            pltpu.VMEM((1, mode_total), f32),
            pltpu.VMEM((1, mode_total), f32),
            pltpu.VMEM(shapes.shape, bf16),
            pltpu.VMEM((shapes.shape[1], shapes.shape[0]), bf16),
            pltpu.VMEM((blocks, 2 * real, depth), bf16),
            pltpu.VMEM((blocks, 2 * real, modes), bf16),
            pltpu.VMEM((blocks, 2 * real, modes), bf16),
            pltpu.VMEM((n_freq, 2 * real_local, modes), bf16),
            pltpu.VMEM((n_freq, 2 * real_local, modes), bf16),
            pltpu.VMEM((blocks, times * real_local, dofs), bf16),
            pltpu.VMEM((blocks, times * real_local, dofs), bf16),
            dma((6,)),
            dma((blocks, PIECES)), dma((blocks, PIECES)),
            dma((blocks, PIECES)), dma((blocks, PIECES)),
            dma((n_freq,)), dma((n_freq,)),
            dma((blocks,)), dma((blocks,)),
        ],
        compiler_params=pltpu.CompilerParams(
            collective_id=0, has_side_effects=True, vmem_limit_bytes=60 * 1024 * 1024
        ),
    )(
        coherency,
        jnp.transpose(phases[0]),
        influence,
        mode_freq.reshape(1, mode_total),
        damping.reshape(1, mode_total),
        shapes,
    )
    return slab.reshape(times, real_local, dofs)


def solution(mesh):
    return jax.shard_map(
        body,
        mesh=mesh,
        in_specs=(
            P("freq", ("support", "row"), None),
            P("freq", ("support", "row"), "group"),
            P(("support", "row"), None),
            P(),
            P(),
            P(None, ("support", "row")),
        ),
        out_specs=P(None, ("group", "freq"), ("support", "row")),
        check_vma=False,
    )
```

```python
import functools
import math

import jax
import jax.numpy as jnp
import numpy as np
from jax import lax
from jax.experimental import pallas as pl
from jax.experimental.pallas import tpu as pltpu
from jax.sharding import PartitionSpec as P

NPH = 64
PIECES = 2
MESH = pl.DeviceIdType.MESH
NT = (((1,), (1,)), ((), ()))
NN = (((1,), (0,)), ((), ()))


def cos_sin(phase):
    quarter = NPH // 4
    quadrant = (phase + quarter // 2) // quarter
    x = (phase - quadrant * quarter).astype(jnp.float32) * (2.0 * math.pi / NPH)
    quadrant = quadrant % 4
    y = x * x
    c = 1.0 + y * (-0.5 + y * (1 / 24 + y * (-1 / 720 + y * (1 / 40320 - y * (1 / 3628800)))))
    s = x * (1.0 + y * (-1 / 6 + y * (1 / 120 + y * (-1 / 5040 + y * (1 / 362880)))))
    odd = (quadrant == 1) | (quadrant == 3)
    cos = jnp.where(odd, s, c)
    sin = jnp.where(odd, c, s)
    cos = jnp.where((quadrant == 1) | (quadrant == 2), -cos, cos)
    sin = jnp.where(quadrant >= 2, -sin, sin)
    return cos, sin


def time_factors(freq_total):
    time_total = 2 * freq_total
    wrapped = np.arange(time_total)[:, None] * (np.arange(freq_total) + 1)[None, :] % time_total
    theta = wrapped * (2.0 * math.pi / time_total)
    scale = math.sqrt(2.0 / freq_total)
    return np.cos(theta) * scale, -np.sin(theta) * scale


def kernel(
    n_support, n_row, n_freq,
    coh_in, ph_in, infl_in, mf_in, dp_in, shp_in,
    out_ref,
    coh, ph, infl, mf, dp, shp,
    shp_t, tab, f_send, f_recv, r_send, r_recv, d_send, d_recv,
    local_sem, a_out, a_in, b_out, b_in, c_out, c_in, d_out, d_in,
):
    blocks = n_support * n_row
    real = ph.shape[0]
    depth = ph.shape[1]
    modes = shp.shape[1]
    real_local = real // n_freq
    dofs = shp.shape[0] // blocks
    my_support, my_row = lax.axis_index("support"), lax.axis_index("row")
    my_freq = lax.axis_index("freq")
    mine = my_support * n_row + my_row

    locals_ = [
        pltpu.make_async_copy(src, dst, local_sem.at[i])
        for i, (src, dst) in enumerate(
            [(ph_in, ph), (mf_in, mf), (dp_in, dp), (coh_in.at[0], coh), (infl_in, infl), (shp_in, shp)]
        )
    ]
    for copy in locals_:
        copy.start()

    def to_block(k):
        return {
            "support": lax.rem(my_support + k // n_row, n_support),
            "row": lax.rem(my_row + k % n_row, n_row),
        }

    def block_to(k):
        at = to_block(k)
        return at["support"] * n_row + at["row"]

    def block_from(k):
        s = lax.rem(my_support + n_support - k // n_row, n_support)
        r = lax.rem(my_row + n_row - k % n_row, n_row)
        return s * n_row + r

    def to_freq(k):
        return {"freq": lax.rem(my_freq + k, n_freq)}

    barrier = pltpu.get_barrier_semaphore()
    for k in range(1, blocks):
        pl.semaphore_signal(barrier, inc=1, device_id=to_block(k), device_id_type=MESH)
    for k in range(1, n_freq):
        pl.semaphore_signal(barrier, inc=1, device_id=to_freq(k), device_id_type=MESH)

    straight = [k for k in range(n_row, blocks) if k % n_row == 0]
    far_first = straight + list(range(1, n_row))
    far_first += [k for k in range(n_row, blocks) if k % n_row]
    near_first = [k for k in range(1, blocks)]

    locals_[0].wait()
    cos, sin = cos_sin(ph[...])
    tab[0] = jnp.concatenate([cos, sin], 0).astype(jnp.bfloat16)

    pl.semaphore_wait(barrier, blocks - 1 + n_freq - 1)

    def send(src, dst, out_sem, in_sem, target):
        copy = pltpu.make_async_remote_copy(
            src_ref=src, dst_ref=dst, send_sem=out_sem, recv_sem=in_sem,
            device_id=target, device_id_type=MESH,
        )
        copy.start()
        return copy

    far = [k for k in far_first if k >= n_row]
    near = [k for k in near_first if k < n_row]
    rows = 2 * real // PIECES
    pieces = [pl.ds(c * rows, rows) for c in range(PIECES)]

    def send_piece(src, dst, k, c, out_sem, in_sem):
        return send(
            src.at[pieces[c]], dst.at[pieces[c]], out_sem.at[k, c], in_sem.at[k, c], to_block(k)
        )

    a_copies = {}
    for c in range(PIECES):
        for k in far_first:
            a_copies[k, c] = send_piece(tab.at[0], tab.at[k], k, c, a_out, a_in)

    locals_[1].wait()
    locals_[2].wait()
    my_modes = pl.ds(pl.multiple_of(mine * modes, modes), modes)
    freq = mf[:, my_modes]
    omega = (my_freq + 1).astype(jnp.float32) * (2.5 / n_freq)
    mode_sq = freq * freq
    real_den = mode_sq - omega * omega
    imag_den = 2.0 * dp[:, my_modes] * freq * omega
    denom = real_den * real_den + imag_den * imag_den
    recep_re = mode_sq * real_den / denom
    recep_im = -mode_sq * imag_den / denom

    def spectra_term(k, part):
        columns = pl.ds(pl.multiple_of(block_from(k) * depth, depth), depth)
        return lax.dot_general(
            tab[k, part], coh[:, columns], NT, preferred_element_type=jnp.float32
        )

    locals_[3].wait()
    whole = pl.ds(0, 2 * real)
    spectra_near = spectra_term(0, whole)
    for k in near:
        for c in range(PIECES):
            a_copies[k, c].wait_recv()
        spectra_near += spectra_term(k, whole)

    def force_term(spectra, k):
        columns = pl.ds(pl.multiple_of(block_to(k) * modes, modes), modes)
        return lax.dot_general(
            spectra, infl[:, columns], NN, preferred_element_type=jnp.float32
        ).astype(jnp.bfloat16)

    b_copies = {}
    forces = []
    for c in range(PIECES):
        spectra = spectra_near[c * rows : (c + 1) * rows]
        for k in far:
            a_copies[k, c].wait_recv()
            spectra += spectra_term(k, pieces[c])
        spectra = spectra.astype(jnp.bfloat16)
        if c == 0:
            locals_[4].wait()
        for k in far_first:
            f_send[k, pieces[c]] = force_term(spectra, k)
            b_copies[k, c] = send_piece(f_send.at[k], f_recv.at[k], k, c, b_out, b_in)
        forces.append(force_term(spectra, 0).astype(jnp.float32))
    locals_[5].wait()
    for b in range(blocks):
        block = slice(b * dofs, (b + 1) * dofs)
        shp_t[:, block] = shp[block, :].T
    def arrived(c):
        total = forces[c]
        for k in near_first:
            b_copies[k, c].wait_recv()
            total += f_recv[k, pieces[c]].astype(jnp.float32)
        return total

    force_re = arrived(0)
    from_re, turned_re = recep_re * force_re, recep_im * force_re
    force_im = arrived(1)
    resp_re = from_re - recep_im * force_im
    resp_im = recep_re * force_im + turned_re
    for f in range(n_freq):
        rows = slice(f * real_local, (f + 1) * real_local)
        r_send[f] = jnp.concatenate([resp_re[rows], resp_im[rows]], 0).astype(jnp.bfloat16)
    c_copies = {
        k: send(
            r_send.at[lax.rem(my_freq + k, n_freq)], r_recv.at[my_freq],
            c_out.at[k], c_in.at[k], to_freq(k),
        )
        for k in range(1, n_freq)
    }
    r_recv[my_freq] = r_send[my_freq]
    for k in range(1, n_freq):
        c_copies[k].wait_recv()

    cos_table, sin_table = time_factors(n_freq)
    parts = [r_recv[f].astype(jnp.float32) for f in range(n_freq)]
    rows = []
    for n in range(2 * n_freq):
        total = None
        for f in range(n_freq):
            term = parts[f][:real_local] * float(cos_table[n, f])
            term += parts[f][real_local:] * float(sin_table[n, f])
            total = term if total is None else total + term
        rows.append(total)
    modal = jnp.concatenate(rows, 0).astype(jnp.bfloat16)

    def slab_term(k):
        block_rows = pl.ds(pl.multiple_of(block_to(k) * dofs, dofs), dofs)
        return lax.dot_general(
            modal, shp_t[:, block_rows], NN, preferred_element_type=jnp.float32
        ).astype(jnp.bfloat16)

    d_copies = {}
    for k in far_first:
        d_send[k] = slab_term(k)
        d_copies[k] = send(d_send.at[k], d_recv.at[k], d_out.at[k], d_in.at[k], to_block(k))
    slab = slab_term(0).astype(jnp.float32)
    for k in near_first:
        d_copies[k].wait_recv()
        slab += d_recv[k].astype(jnp.float32)
    out_ref[...] = slab

    for copies in (a_copies, b_copies, c_copies, d_copies):
        for copy in copies.values():
            copy.wait_send()


def body(coherency, phases, influence, mode_freq, damping, shapes):
    n_support, n_row = lax.axis_size("support"), lax.axis_size("row")
    n_freq = lax.axis_size("freq")
    blocks = n_support * n_row
    depth, real = phases.shape[1], phases.shape[2]
    mode_total, modes = influence.shape[1], shapes.shape[1]
    dofs = shapes.shape[0] // blocks
    real_local = real // n_freq
    times = 2 * n_freq
    bf16, f32 = jnp.bfloat16, jnp.float32
    dma = pltpu.SemaphoreType.DMA
    slab = pl.pallas_call(
        functools.partial(kernel, n_support, n_row, n_freq),
        out_shape=jax.ShapeDtypeStruct((times * real_local, dofs), f32),
        in_specs=[pl.BlockSpec(memory_space=pltpu.HBM)] * 6,
        out_specs=pl.BlockSpec(memory_space=pltpu.VMEM),
        scratch_shapes=[
            pltpu.VMEM(coherency.shape[1:], bf16),
            pltpu.VMEM((real, depth), jnp.int32),
            pltpu.VMEM(influence.shape, bf16),
            pltpu.VMEM((1, mode_total), f32),
            pltpu.VMEM((1, mode_total), f32),
            pltpu.VMEM(shapes.shape, bf16),
            pltpu.VMEM((shapes.shape[1], shapes.shape[0]), bf16),
            pltpu.VMEM((blocks, 2 * real, depth), bf16),
            pltpu.VMEM((blocks, 2 * real, modes), bf16),
            pltpu.VMEM((blocks, 2 * real, modes), bf16),
            pltpu.VMEM((n_freq, 2 * real_local, modes), bf16),
            pltpu.VMEM((n_freq, 2 * real_local, modes), bf16),
            pltpu.VMEM((blocks, times * real_local, dofs), bf16),
            pltpu.VMEM((blocks, times * real_local, dofs), bf16),
            dma((6,)),
            dma((blocks, PIECES)), dma((blocks, PIECES)),
            dma((blocks, PIECES)), dma((blocks, PIECES)),
            dma((n_freq,)), dma((n_freq,)),
            dma((blocks,)), dma((blocks,)),
        ],
        compiler_params=pltpu.CompilerParams(
            collective_id=0, has_side_effects=True, vmem_limit_bytes=60 * 1024 * 1024
        ),
    )(
        coherency,
        jnp.transpose(phases[0]),
        influence,
        mode_freq.reshape(1, mode_total),
        damping.reshape(1, mode_total),
        shapes,
    )
    return slab.reshape(times, real_local, dofs)


def solution(mesh):
    return jax.shard_map(
        body,
        mesh=mesh,
        in_specs=(
            P("freq", ("support", "row"), None),
            P("freq", ("support", "row"), "group"),
            P(("support", "row"), None),
            P(),
            P(),
            P(None, ("support", "row")),
        ),
        out_specs=P(None, ("group", "freq"), ("support", "row")),
        check_vma=False,
    )
```
